512 devices in a mesh: row: 32 (over x_hi, y, core), col: 16 (over x_lo, z).
Axes of the slice: x: 4 (x_hi: 2, x_lo: 2; x = x_hi * 2 + x_lo), y: 8, z: 8, core: 2. Of those that a mesh axis runs over, the one named last changes fastest.
Arguments:
- prior: bfloat16 [65536, 256], P(('row', 'col')), may hold values from 0.1 to 2
- inv_degree: float32 [65536], P(('row', 'col')), may hold values from 0.03125 to 0.125
- seed_rows: int32 [8192], P(('row', 'col')), may hold values from 0 to 127, as said below
- seed_scores: bfloat16 [8192, 256], P(('row', 'col')), may hold values from 0.1 to 2
- block_mask: int32 [36864, 128, 128], P(('row', 'col')), may hold values 0 or 1
- block_row: int32 [36864], P(('row', 'col')), may hold values from 0 to 31, as said below
- block_col: int32 [36864], P(('row', 'col')), may hold values from 0 to 15, as said below
- block_live: int32 [512], P(('row', 'col')), may hold values from 9 to 72, as said below
Outputs:
- labels: bfloat16 [65536, 256], P(('row', 'col'))
The draws below stay inside these ranges and needn't reach their ends.
Inputs may be any that keep to these rules, and one draw needn't show every extreme that they name: `seed_rows`: within one device's 16 entries the indices are distinct. Within one device's 72 slots, the pairs (block_row, block_col) are distinct. `block_col`: see block_row. `block_live`: some device uses all 72 slots.
All inputs are finite; a program needn't handle non-finite values. No bound on the sum of `block_mask` on one device may be relied on, other than what follows from the above.
Results may differ from the reference program's by a relative error of at most 0.015.
Values may be sent and summed in bfloat16 or wider, within the bound.
A program may use at most 64 MiB of HBM per device.

```python
import math
import jax
import jax.numpy as jnp
from jax import lax

L = 256
BLK = 128
ITERS = 2
DOCS_DEV = 128
DOCS = 65536
TBR = 32
TBC = 16
SLOTS = 72
SEEDS_DEV = 16
N_ROW = 32
N_COL = 16


LOW_SCORE = 0.1


HIGH_SCORE = 2.0


def pattern_slots(key):
    inner = jax.random.fold_in(key, 11)
    keys = jax.random.split(inner, N_ROW * N_COL)
    perms = jax.vmap(lambda single: jax.random.permutation(single, TBR * TBC))(keys)
    return perms[:, :SLOTS].astype(jnp.int32)


def draw_block_row(key, part):
    return (pattern_slots(key) // TBC).reshape(-1).astype(jnp.int32)


def draw_block_col(key, part):
    return (pattern_slots(key) % TBC).reshape(-1).astype(jnp.int32)


def draw_block_live(key, part):
    inner = jax.random.fold_in(key, 23)
    first, second = jax.random.split(inner)
    shifts = jax.random.randint(first, (N_ROW * N_COL,), 0, 4)
    counts = SLOTS // jnp.left_shift(jnp.ones_like(shifts), shifts)
    chosen = jax.random.randint(second, (), 0, N_ROW * N_COL)
    counts = jnp.where(jnp.arange(N_ROW * N_COL) == chosen, SLOTS, counts)
    return counts.astype(jnp.int32)


def draw_seed_rows(key, part):
    inner = jax.random.fold_in(key, 37)
    keys = jax.random.split(inner, N_ROW * N_COL)
    perms = jax.vmap(lambda single: jax.random.permutation(single, DOCS_DEV))(keys)
    return perms[:, :SEEDS_DEV].reshape(-1).astype(jnp.int32)


def label_levels(key):
    inner = jax.random.fold_in(key, 61)
    first, second = jax.random.split(inner)
    column = jax.random.uniform(first, (L,), jnp.float32)
    groups = jax.random.uniform(second, (16,), jnp.float32)
    group = jnp.repeat(groups, L // 16)
    return (column, group)


def to_score(mixed):
    value = jnp.exp(jnp.log(LOW_SCORE) + mixed * jnp.log(HIGH_SCORE / LOW_SCORE))
    return jnp.clip(value, LOW_SCORE, HIGH_SCORE).astype(jnp.float32)


def draw_prior(key, part):
    column, group = label_levels(key)
    inner = jax.random.fold_in(key, 67)
    noise = jax.random.uniform(inner, (DOCS, L), jnp.float32)
    mixed = 0.15 * column[None, :] + 0.1 * group[None, :] + 0.75 * noise
    return to_score(mixed).astype(jnp.bfloat16)


def draw_seed_scores(key, part):
    column, group = label_levels(key)
    inner = jax.random.fold_in(key, 71)
    noise = jax.random.uniform(inner, (N_ROW * N_COL * SEEDS_DEV, L), jnp.float32)
    mixed = 0.15 * column[None, :] + 0.1 * group[None, :] + 0.75 * noise
    return to_score(mixed).astype(jnp.bfloat16)


def with_ends(drawn, stream_key, least, high):
    longest = drawn.shape.index(max(drawn.shape))
    spots = []
    for shift in (0, 1):
        where = [jax.random.randint(jax.random.fold_in(stream_key, axis), (), 0, length) for axis, length in enumerate(drawn.shape)]
        where[longest] = (where[longest] + shift) % drawn.shape[longest]
        spots.append(tuple(where))
    return drawn.at[spots[0]].set(least).at[spots[1]].set(high)


def levels(key, shape, pieces, low, high):
    factor_of, own = 1.0, jax.random.fold_in(key, 6)
    for dim, blocks in pieces:
        draws = jnp.exp(jax.random.uniform(jax.random.fold_in(own, dim), (blocks,), jnp.float32, low / len(pieces), high / len(pieces)))
        factor_of = factor_of * jnp.repeat(draws, shape[dim] // blocks).reshape([-1 if axis == dim else 1 for axis in range(len(shape))])
    return factor_of


def setup_inputs(seed: int = 0) -> dict:
    arg_keys = jax.random.split(jax.random.key(seed), 9)
    return {
        "prior": draw_prior(jax.random.fold_in(arg_keys[8], 71), 0),
        "inv_degree": jnp.clip(jnp.exp(math.log(0.125) - 1.3862944 * jax.random.uniform(arg_keys[1], (DOCS,), jnp.float32) ** levels(arg_keys[1], (DOCS,), ((0, 512),), -0.2, 0.2)), 0.03125, 0.125),
        "seed_rows": draw_seed_rows(jax.random.fold_in(arg_keys[8], 71), 0),
        "seed_scores": draw_seed_scores(jax.random.fold_in(arg_keys[8], 71), 0),
        "block_mask": with_ends((jax.random.randint(arg_keys[4], (N_ROW * N_COL * SLOTS, BLK, BLK), 0, SLOTS * BLK * BLK // (32 * DOCS_DEV)) < 1).astype(jnp.int32), jax.random.fold_in(arg_keys[4], 1), 0, 1),
        "block_row": draw_block_row(jax.random.fold_in(arg_keys[8], 71), 0),
        "block_col": draw_block_col(jax.random.fold_in(arg_keys[8], 71), 0),
        "block_live": draw_block_live(jax.random.fold_in(arg_keys[8], 71), 0),
    }


MIX_RATE = 0.9


def reference(prior, inv_degree, seed_rows, seed_scores, block_mask, block_row, block_col, block_live):
    devices = N_ROW * N_COL
    masks = block_mask.reshape(devices, SLOTS, BLK, BLK)
    rows_all = block_row.reshape(devices, SLOTS)
    cols_all = block_col.reshape(devices, SLOTS)
    slot_ids = jnp.arange(SLOTS, dtype=jnp.int32)
    block_ids = jnp.arange(TBR, dtype=jnp.int32)
    seed_index = (jnp.arange(devices, dtype=jnp.int32)[:, None] * DOCS_DEV + seed_rows.reshape(devices, SEEDS_DEV)).reshape(-1).astype(jnp.int32)
    base = (1.0 - MIX_RATE) * prior.astype(jnp.float32)
    labels = prior
    for step in range(ITERS):
        grid = labels.reshape(N_ROW, N_COL * DOCS_DEV, L)

        def per_col(c):
            def per_row(acc, r):
                q = (r * N_COL + c).astype(jnp.int32)
                mask_q = lax.dynamic_index_in_dim(masks, q, keepdims=False)
                live_q = lax.dynamic_index_in_dim(block_live, q, keepdims=False)
                rows_q = lax.dynamic_index_in_dim(rows_all, q, keepdims=False)
                cols_q = lax.dynamic_index_in_dim(cols_all, q, keepdims=False)
                weights = (mask_q * (slot_ids < live_q).astype(jnp.int32)[:, None, None]).astype(jnp.float32)
                src_all = lax.dynamic_index_in_dim(grid, r, keepdims=False).reshape(TBC, BLK, L)
                src = jnp.take(src_all, cols_q, axis=0).astype(jnp.float32)
                out = jnp.einsum("sij,sjl->sil", weights, src, precision=lax.Precision.HIGHEST)
                hot = (rows_q[:, None] == block_ids[None, :]).astype(jnp.float32)
                part = jnp.einsum("st,sbl->tbl", hot, out, precision=lax.Precision.HIGHEST)
                part = lax.optimization_barrier(part.astype(jnp.bfloat16)).astype(jnp.float32)
                return acc + part, None

            acc, unused = lax.scan(per_row, jnp.zeros((TBR, BLK, L), jnp.float32), jnp.arange(N_ROW, dtype=jnp.int32))
            return acc

        sums = lax.map(per_col, jnp.arange(N_COL, dtype=jnp.int32))
        sums = sums.reshape(N_COL, N_ROW, DOCS_DEV, L).transpose(1, 0, 2, 3).reshape(DOCS, L)
        fresh = MIX_RATE * inv_degree[:, None] * sums + base
        fresh = fresh.at[seed_index].set(seed_scores.astype(jnp.float32))
        labels = fresh.astype(jnp.bfloat16)
    return labels
```

```python
import functools

import jax
import jax.numpy as jnp
from jax import lax
from jax.experimental import pallas as pl
from jax.experimental.pallas import tpu as pltpu
from jax.sharding import PartitionSpec as P

ITERS = 2
MIX_RATE = 0.9
BLK = 128
HALF = 128
HALVES = 2
NZ, NY = 8, 8
LEAD = 0

ROUNDS = (
    (("P", (0, 0), (0, -1)), ("N", (0, 0), (0, 1)), ("X", (0, 0), (1, 0))),
    (("P", (0, -1), (0, -2)), ("N", (0, 1), (0, 2)), ("X", (0, 1), (1, 1))),
    (("P", (0, -2), (0, -3)), ("N", (0, 2), (0, 3)), ("X", (0, 2), (1, 2))),
    (("P", (0, -3), (0, -4)), ("N", (1, 2), (1, 3)), ("X", (0, -2), (1, -2))),
    (("P", (1, -2), (1, -3)), ("N", (1, 3), (1, 4)), ("X", (0, -1), (1, -1))),
)
ORDER = (4, 3, -3, 2, -2, 1, -1, 0)
MCHUNKS = 4


def slot(pos):
    return (pos[0] * NZ + pos[1] % NZ) * BLK


def at(j):
    return ORDER.index(j) * 2 * BLK


def kernel(
    prior_ref, inv_ref, seed_rows_ref, seed_scores_ref, mask_hbm, brow_ref, bcol_ref, live_ref,
    out_ref,
    mask_v, wblk, weights, src, csend, crecv, own, ysend, yrecv, xsend, xrecv,
    base, factor, covered, table_v, table_s, send_sem, recv_sem, local_sem,
):
    row, col = lax.axis_index("row"), lax.axis_index("col")
    core = row % 2
    y = (row // 2) % NY
    xh = row // (2 * NY)
    z = col % NZ
    xl = col // NZ
    slots = mask_v.shape[0]

    def rowof(a, b, c):
        return (a * NY + b) * 2 + c

    peers = {
        "P": (row, xl * NZ + (z + 1) % NZ),
        "N": (row, xl * NZ + (z + NZ - 1) % NZ),
        "X": (row, (1 - xl) * NZ + z),
        "C": (rowof(xh, y, 1 - core), col),
        "U": (rowof(xh, (y + 1) % NY, core), col),
        "D": (rowof(xh, (y + NY - 1) % NY, core), col),
        "H": (rowof(1 - xh, y, core), col),
    }

    mask_copy = pltpu.make_async_copy(mask_hbm, mask_v, local_sem.at[0])
    mask_copy.start()

    barrier = pltpu.get_barrier_semaphore()
    for peer in peers.values():
        pl.semaphore_signal(barrier, inc=1, device_id=peer, device_id_type=pl.DeviceIdType.MESH)

    for h in range(HALVES):
        src[0, h, 0:BLK, :] = prior_ref[:, h * HALF : (h + 1) * HALF]

    pl.semaphore_wait(barrier, len(peers))

    started = []

    def send(source, target, peer):
        n = len(started)
        copy = pltpu.make_async_remote_copy(
            src_ref=source,
            dst_ref=target,
            send_sem=send_sem.at[n],
            recv_sem=recv_sem.at[n],
            device_id=peers[peer],
            device_id_type=pl.DeviceIdType.MESH,
        )
        copy.start()
        started.append(copy)
        return copy

    def prepare():
        spot = lax.broadcasted_iota(jnp.int32, (8, 128), 0) * 128 + lax.broadcasted_iota(
            jnp.int32, (8, 128), 1
        )
        live = live_ref[0]

        def mark(s, acc):
            key = brow_ref[s] * (2 * NZ) + bcol_ref[s]
            key = jnp.where(s < live, key, -1)
            return jnp.where(spot == key, s + 1, acc)

        table_v[...] = lax.fori_loop(0, slots, mark, jnp.zeros((8, 128), jnp.int32))
        table_copy = pltpu.make_async_copy(table_v, table_s, local_sem.at[1])
        table_copy.start()

        docs = lax.broadcasted_iota(jnp.int32, (BLK, seed_rows_ref.shape[1]), 0)
        hits = (docs == seed_rows_ref[...]).astype(jnp.float32)
        seeded = jnp.dot(
            hits.astype(jnp.bfloat16), seed_scores_ref[...], preferred_element_type=jnp.float32
        )
        cov = jnp.broadcast_to(jnp.sum(hits, axis=1, keepdims=True), (BLK, HALF))
        covered[...] = cov
        eye = lax.broadcasted_iota(jnp.int32, (BLK, BLK), 0) == lax.broadcasted_iota(
            jnp.int32, (BLK, BLK), 1
        )
        inv = jnp.sum(jnp.where(eye, inv_ref[...], 0.0), axis=1, keepdims=True)
        factor[...] = jnp.broadcast_to(MIX_RATE * inv, (BLK, HALF))
        for h in range(HALVES):
            cols = slice(h * HALF, (h + 1) * HALF)
            base[h] = jnp.where(
                cov > 0.5,
                seeded[:, cols],
                (1.0 - MIX_RATE) * prior_ref[:, cols].astype(jnp.float32),
            )
        mask_copy.wait()
        wblk[0] = jnp.zeros((BLK, BLK), jnp.bfloat16)

        @pl.loop(0, slots)
        def _(s):
            wblk[s + 1] = mask_v[s].astype(jnp.float32).astype(jnp.bfloat16)

        table_copy.wait()

    def build(first, last):
        @pl.loop(first, last)
        def _(rb):
            kk = rb // 16
            p = (rb // 2) % 8
            xx = rb % 2
            j = (4 - (p + 1) // 2) * (2 * (p % 2) - 1)
            b = rowof((xh + 1 + xx) % 2, (y + j + NY) % NY, (core + 1 + kk) % 2)
            for dx in range(2):
                for dz in range(NZ):
                    c = ((xl + dx) % 2) * NZ + (z + dz) % NZ
                    which = table_s[b // 8, (b % 8) * 16 + c]
                    weights[
                        pl.ds(pl.multiple_of(rb * BLK, BLK), BLK),
                        (dx * NZ + dz) * BLK : (dx * NZ + dz + 1) * BLK,
                    ] = wblk[which]

    def flow(it, h):
        arrived = {}
        for n, steps in enumerate(ROUNDS):
            for way, here, there in steps:
                if here in arrived:
                    arrived.pop(here).wait_recv()
                arrived[there] = send(
                    src.at[it, h, pl.ds(slot(here), BLK)],
                    src.at[it, h, pl.ds(slot(there), BLK)],
                    way,
                )
            if it == 0 and h == 0:
                if n == 0:
                    prepare()
                else:
                    build((n - 1) * 8, n * 8)
            yield
        for copy in arrived.values():
            copy.wait_recv()
        labels = src.at[it, h]
        rows = 2 * NY * BLK // MCHUNKS
        core_copies = []
        for m in range(MCHUNKS):
            part = jnp.dot(
                weights[m * rows : (m + 1) * rows, :],
                labels[...],
                preferred_element_type=jnp.float32,
            )
            csend[it, h, m * rows : (m + 1) * rows, :] = part.astype(jnp.bfloat16)
            where = pl.ds(m * rows, rows)
            core_copies.append(send(csend.at[it, h, where], crecv.at[it, h, where], "C"))
            yield
        for m in range(MCHUNKS):
            first = 2 * NY * BLK + m * rows
            own[h, m * rows : (m + 1) * rows, :] = jnp.dot(
                weights[first : first + rows, :],
                labels[...],
                preferred_element_type=jnp.float32,
            )
            yield

        waited = set()

        def local(j, xx, n=1):
            first = at(j) + xx * BLK
            m = first // rows
            if m not in waited:
                waited.add(m)
                core_copies[m].wait_recv()
            where = slice(first, first + n * BLK)
            return own[h, where, :] + crecv[it, h, where, :].astype(jnp.float32)

        up, down = ysend.at[it, h, 0], ysend.at[it, h, 1]
        rup, rdown = yrecv.at[it, h, 0], yrecv.at[it, h, 1]
        one, both = pl.ds(0, BLK), pl.ds(0, 2 * BLK)
        up[0, 0:BLK, :] = local(4, 0).astype(jnp.bfloat16)
        u = send(up.at[0, one], rup.at[0, one], "U")
        down[0, 0:BLK, :] = local(4, 1).astype(jnp.bfloat16)
        d = send(down.at[0, one], rdown.at[0, one], "D")
        yield
        for step in (1, 2, 3):
            j = 4 - step
            if step == 1:
                up[1, BLK:, :] = local(j, 1).astype(jnp.bfloat16)
                down[1, 0:BLK, :] = local(-j, 0).astype(jnp.bfloat16)
                u.wait_recv()
                up[1, 0:BLK, :] = (local(j, 0) + rup[0, 0:BLK, :].astype(jnp.float32)).astype(
                    jnp.bfloat16
                )
            else:
                u.wait_recv()
                up[step] = (local(j, 0, 2) + rup[step - 1].astype(jnp.float32)).astype(jnp.bfloat16)
            u = send(up.at[step, both], rup.at[step, both], "U")
            d.wait_recv()
            if step == 1:
                down[1, BLK:, :] = (local(-j, 1) + rdown[0, 0:BLK, :].astype(jnp.float32)).astype(
                    jnp.bfloat16
                )
            else:
                down[step] = (local(-j, 0, 2) + rdown[step - 1].astype(jnp.float32)).astype(
                    jnp.bfloat16
                )
            d = send(down.at[step, both], rdown.at[step, both], "D")
            yield
        u.wait_recv()
        d.wait_recv()
        pieces = [
            local(0, xx)
            + rup[3, xx * BLK : (xx + 1) * BLK, :].astype(jnp.float32)
            + rdown[3, xx * BLK : (xx + 1) * BLK, :].astype(jnp.float32)
            for xx in (0, 1)
        ]
        xsend[it, h] = pieces[0].astype(jnp.bfloat16)
        x = send(xsend.at[it, h], xrecv.at[it, h], "H")
        own[h, at(0) + BLK : at(0) + 2 * BLK, :] = pieces[1]
        yield
        x.wait_recv()
        total = own[h, at(0) + BLK : at(0) + 2 * BLK, :] + xrecv[it, h].astype(jnp.float32)
        mixed = jnp.where(covered[...] > 0.5, base[h], factor[...] * total + base[h])
        if it == ITERS - 1:
            out_ref[:, h * HALF : (h + 1) * HALF] = mixed.astype(jnp.bfloat16)
        else:
            src[it + 1, h, 0:BLK, :] = mixed.astype(jnp.bfloat16)

    def stream(h):
        for it in range(ITERS):
            yield from flow(it, h)

    streams = [stream(h) for h in range(HALVES)]
    done = object()
    for _ in range(LEAD):
        next(streams[0])
    while streams:
        streams = [s for s in streams if next(s, done) is not done]
    for copy in started:
        copy.wait_send()


COPIES = 28 * ITERS * HALVES


def local(prior, inv_degree, seed_rows, seed_scores, block_mask, block_row, block_col, block_live):
    slots = block_mask.shape[0]
    vmem = pl.BlockSpec(memory_space=pltpu.VMEM)
    smem = pl.BlockSpec(memory_space=pltpu.SMEM)
    bf16, f32 = jnp.bfloat16, jnp.float32
    targets, sources = 4 * NY * BLK, 2 * NZ * BLK
    return pl.pallas_call(
        kernel,
        out_shape=jax.ShapeDtypeStruct(prior.shape, bf16),
        in_specs=[vmem, vmem, vmem, vmem, pl.BlockSpec(memory_space=pl.ANY), smem, smem, smem],
        out_specs=vmem,
        scratch_shapes=[
            pltpu.VMEM((slots, BLK, BLK), jnp.int32),
            pltpu.VMEM((slots + 1, BLK, BLK), bf16),
            pltpu.VMEM((targets, sources), bf16),
            pltpu.VMEM((ITERS, HALVES, sources, HALF), bf16),
            pltpu.VMEM((ITERS, HALVES, targets // 2, HALF), bf16),
            pltpu.VMEM((ITERS, HALVES, targets // 2, HALF), bf16),
            pltpu.VMEM((HALVES, targets // 2, HALF), f32),
            pltpu.VMEM((ITERS, HALVES, 2, 4, 2 * BLK, HALF), bf16),
            pltpu.VMEM((ITERS, HALVES, 2, 4, 2 * BLK, HALF), bf16),
            pltpu.VMEM((ITERS, HALVES, BLK, HALF), bf16),
            pltpu.VMEM((ITERS, HALVES, BLK, HALF), bf16),
            pltpu.VMEM((HALVES, BLK, HALF), f32),
            pltpu.VMEM((BLK, HALF), f32),
            pltpu.VMEM((BLK, HALF), f32),
            pltpu.VMEM((8, 128), jnp.int32),
            pltpu.SMEM((8, 128), jnp.int32),
            pltpu.SemaphoreType.DMA((COPIES,)),
            pltpu.SemaphoreType.DMA((COPIES,)),
            pltpu.SemaphoreType.DMA((2,)),
        ],
        compiler_params=pltpu.CompilerParams(
            collective_id=0, has_side_effects=True, vmem_limit_bytes=56 * 1024 * 1024
        ),
        name="propagate",
    )(
        prior,
        inv_degree.reshape(1, -1),
        seed_rows.reshape(1, -1),
        seed_scores,
        block_mask,
        block_row,
        block_col,
        block_live,
    )


def solution(mesh):
    return jax.shard_map(
        local,
        mesh=mesh,
        in_specs=(
            P(("row", "col"), None),
            P(("row", "col")),
            P(("row", "col")),
            P(("row", "col"), None),
            P(("row", "col"), None, None),
            P(("row", "col")),
            P(("row", "col")),
            P(("row", "col")),
        ),
        out_specs=P(("row", "col"), None),
        check_vma=False,
    )
```

```python
import jax
import jax.numpy as jnp
from jax import lax
from jax.experimental import pallas as pl
from jax.experimental.pallas import tpu as pltpu
from jax.sharding import PartitionSpec as P

ITERS = 2
MIX_RATE = 0.9
BLK = 128
NZ, NY = 8, 8

GROUPS = (
    ((0, 0), (0, 2), (0, 6), (1, 0), (0, 1), (0, 7)),
    ((0, 3), (0, 5), (1, 2), (1, 6), (1, 1), (1, 7)),
    ((0, 4), (1, 3), (1, 5), (1, 4)),
)
SLOTS = sum(GROUPS, ())
ORDER = (4, 3, -3, 2, -2, 1, -1, 0)
PIECES = len(ORDER) * BLK
ROWS = 512


def slot(dx, dz):
    return SLOTS.index((dx, dz % NZ)) * BLK


def kernel(
    prior_ref, inv_ref, seed_rows_ref, seed_scores_ref, mask_hbm, brow_ref, bcol_ref, live_ref,
    out_ref,
    mask_v, wblk, weights, src, csend, crecv, acc, ysend, yrecv, xsend, xrecv, mine,
    base, factor, covered, table_v, table_s, send_sem, recv_sem, local_sem,
):
    f32, bf16 = jnp.float32, jnp.bfloat16
    width = prior_ref.shape[1]
    row, col = lax.axis_index("row"), lax.axis_index("col")
    core = row % 2
    y = (row // 2) % NY
    xh = row // (2 * NY)
    z = col % NZ
    xl = col // NZ
    slots = mask_v.shape[0]

    def rowof(a, b, c):
        return (a * NY + b) * 2 + c

    def along_z(d):
        return (row, xl * NZ + (z + d + NZ) % NZ)

    def along_y(d):
        return (rowof(xh, (y + d + NY) % NY, core), col)

    peers = {
        "X": (row, (1 - xl) * NZ + z),
        "C": (rowof(xh, y, 1 - core), col),
        "H": (rowof(1 - xh, y, core), col),
    }
    for d in (1, 2, -1, -2):
        peers["z", d] = along_z(d)
        peers["y", d] = along_y(d)

    mask_copy = pltpu.make_async_copy(mask_hbm, mask_v, local_sem.at[0])
    mask_copy.start()

    barrier = pltpu.get_barrier_semaphore()
    for peer in peers.values():
        pl.semaphore_signal(barrier, inc=1, device_id=peer, device_id_type=pl.DeviceIdType.MESH)

    src[0, slot(0, 0) : slot(0, 0) + BLK, :] = prior_ref[...]

    started = []

    def send(source, target, peer):
        n = len(started)
        copy = pltpu.make_async_remote_copy(
            src_ref=source,
            dst_ref=target,
            send_sem=send_sem.at[n],
            recv_sem=recv_sem.at[n],
            device_id=peers[peer],
            device_id_type=pl.DeviceIdType.MESH,
        )
        copy.start()
        started.append(copy)
        return copy

    def prepare_table():
        spot = lax.broadcasted_iota(jnp.int32, (8, 128), 0) * 128 + lax.broadcasted_iota(
            jnp.int32, (8, 128), 1
        )
        live = live_ref[0]

        def mark(s, table):
            key = brow_ref[s] * (2 * NZ) + bcol_ref[s]
            key = jnp.where(s < live, key, -1)
            return jnp.where(spot == key, s + 1, table)

        table_v[...] = lax.fori_loop(0, slots, mark, jnp.zeros((8, 128), jnp.int32))
        copy = pltpu.make_async_copy(table_v, table_s, local_sem.at[1])
        copy.start()
        return copy

    def prepare_labels():
        docs = lax.broadcasted_iota(jnp.int32, (BLK, seed_rows_ref.shape[1]), 0)
        hits = (docs == seed_rows_ref[...]).astype(f32)
        seeded = jnp.dot(hits.astype(bf16), seed_scores_ref[...], preferred_element_type=f32)
        cov = jnp.broadcast_to(jnp.sum(hits, axis=1, keepdims=True), (BLK, width))
        covered[...] = cov
        eye = lax.broadcasted_iota(jnp.int32, (BLK, BLK), 0) == lax.broadcasted_iota(
            jnp.int32, (BLK, BLK), 1
        )
        inv = jnp.sum(jnp.where(eye, inv_ref[...], 0.0), axis=1, keepdims=True)
        factor[...] = jnp.broadcast_to(MIX_RATE * inv, (BLK, width))
        base[...] = jnp.where(cov > 0.5, seeded, (1.0 - MIX_RATE) * prior_ref[...].astype(f32))

    def convert():
        mask_copy.wait()
        wblk[0] = jnp.zeros((BLK, BLK), bf16)

        @pl.loop(0, slots)
        def _(s):
            wblk[s + 1] = mask_v[s].astype(f32).astype(bf16)

    def build(group):
        @pl.loop(0, 4)
        def _(q):
            kk = q // 2
            xx = q % 2
            for p, j in enumerate(ORDER):
                b = rowof((xh + 1 + xx) % 2, (y + j + NY) % NY, (core + 1 + kk) % 2)
                first = pl.multiple_of(q * PIECES + p * BLK, BLK)
                for dx, dz in group:
                    c = ((xl + dx) % 2) * NZ + (z + dz) % NZ
                    which = table_s[b // 8, (b % 8) * 16 + c]
                    weights[pl.ds(first, BLK), slot(dx, dz) : slot(dx, dz) + BLK] = wblk[which]

    def product(it, n, first):
        k = slot(*GROUPS[n][0])
        depth = len(GROUPS[n]) * BLK
        return jnp.dot(
            weights[first : first + ROWS, k : k + depth],
            src[it, k : k + depth, :],
            preferred_element_type=f32,
        )

    def products(it, n):
        for first in range(0, 4 * PIECES, ROWS):
            part = product(it, n, first)
            if n:
                part = part + acc[first : first + ROWS, :]
            acc[first : first + ROWS, :] = part

    half = BLK // 2
    table_copy = prepare_table()
    prepare_labels()
    pl.semaphore_wait(barrier, len(peers))

    for it in range(ITERS):
        coming = {}

        def block(pos, part):
            return src.at[it, pl.ds(slot(*pos) + part * half, half)]

        def take(dx, dz, part):
            copy = coming.pop((dx, dz % NZ, part), None)
            if copy is not None:
                copy.wait_recv()

        def pass_on(dx, dz, part, way, there):
            take(dx, dz, part)
            coming[there[0], there[1] % NZ, part] = send(
                block((dx, dz), part), block(there, part), way
            )

        for part in (0, 1):
            pass_on(0, 0, part, ("z", 2), (0, -2))
            pass_on(0, 0, part, ("z", -2), (0, 2))
            pass_on(0, 0, part, "X", (1, 0))
        for part in (0, 1):
            pass_on(0, 0, part, ("z", 1), (0, -1))
            pass_on(0, 0, part, ("z", -1), (0, 1))
        if it == 0:
            convert()
        for part in (0, 1):
            for d in (-2, 2):
                s = -1 if d > 0 else 1
                pass_on(0, d, part, "X", (1, d))
                pass_on(0, d, part, ("z", s), (0, d - s))
                if (part == 0) == (d < 0):
                    pass_on(0, d, part, ("z", 2 * s), (0, 4))
        for part in (0, 1):
            for d in (-1, 1):
                pass_on(0, d, part, "X", (1, d))
        if it == 0:
            table_copy.wait()
            build(GROUPS[0] + GROUPS[1])
        else:
            for part in (0, 1):
                take(1, 0, part)
            products(it, 0)
        for part in (0, 1):
            for d in (-2, 2):
                s = -1 if d > 0 else 1
                pass_on(1, d, part, ("z", s), (1, d - s))
                if (part == 0) == (d > 0):
                    pass_on(1, d, part, ("z", 2 * s), (1, 4))
        if it == 0:
            for part in (0, 1):
                take(1, 0, part)
            products(it, 0)
            build(GROUPS[2])
        for dx, dz in GROUPS[1]:
            for part in (0, 1):
                take(dx, dz, part)
        products(it, 1)
        for dx, dz in GROUPS[2]:
            for part in (0, 1):
                take(dx, dz, part)

        core_copies = {}

        def finish(kk, xx):
            for first in range(xx * PIECES, (xx + 1) * PIECES, ROWS):
                at = kk * 2 * PIECES + first
                part = product(it, 2, at) + acc[at : at + ROWS, :]
                if kk:
                    acc[at : at + ROWS, :] = part
                else:
                    csend[it, first : first + ROWS, :] = part.astype(bf16)
                    where = pl.ds(first, ROWS)
                    core_copies[first // ROWS] = send(
                        csend.at[it, where], crecv.at[it, where], "C"
                    )

        def local(j, xx, top=0, rows=BLK):
            first = xx * PIECES + ORDER.index(j) * BLK + top
            copy = core_copies.pop(first // ROWS, None)
            if copy is not None:
                copy.wait_recv()
            at = 2 * PIECES + first
            return acc[at : at + rows, :] + crecv[it, first : first + rows, :].astype(f32)

        sent = {}

        def ship(n, xx, value, way, rows=BLK):
            ysend[it, xx, n, 0:rows, :] = value.astype(bf16)
            where = pl.ds(0, rows)
            sent[n, xx] = send(ysend.at[it, xx, n, where], yrecv.at[it, xx, n, where], way)

        def landed(n, xx, rows=BLK):
            sent.pop((n, xx)).wait_recv()
            return yrecv[it, xx, n, 0:rows, :].astype(f32)

        def far(xx):
            ship(0, xx, local(4, xx, 0, half), ("y", 2), half)
            ship(1, xx, local(4, xx, half, half), ("y", -2), half)
            ship(2, xx, local(3, xx), ("y", 1))
            ship(3, xx, local(-3, xx), ("y", -1))

        def near(xx):
            ship(4, xx, local(1, xx), ("y", 1))
            ship(5, xx, local(-1, xx), ("y", -1))

        def middle(xx):
            total = local(2, xx) + landed(2, xx)
            ship(
                6, xx,
                jnp.concatenate([total[:half] + landed(0, xx, half), total[half:]], axis=0),
                ("y", 2),
            )
            total = local(-2, xx) + landed(3, xx)
            ship(
                7, xx,
                jnp.concatenate([total[:half], total[half:] + landed(1, xx, half)], axis=0),
                ("y", -2),
            )

        def gathered(xx):
            total = local(0, xx)
            for n in (4, 5, 6, 7):
                total = total + landed(n, xx)
            return total

        finish(0, 0)
        finish(1, 0)
        far(0)
        finish(0, 1)
        finish(1, 1)
        far(1)
        near(0)
        middle(0)
        near(1)
        middle(1)
        xsend[it] = gathered(0).astype(bf16)
        across = send(xsend.at[it], xrecv.at[it], "H")
        mine[...] = gathered(1)
        across.wait_recv()
        total = mine[...] + xrecv[it].astype(f32)
        mixed = jnp.where(covered[...] > 0.5, base[...], factor[...] * total + base[...])
        if it == ITERS - 1:
            out_ref[...] = mixed.astype(bf16)
        else:
            src[it + 1, slot(0, 0) : slot(0, 0) + BLK, :] = mixed.astype(bf16)

    for copy in started:
        copy.wait_send()


COPIES = (30 + 4 + 16 + 1) * ITERS


def local(prior, inv_degree, seed_rows, seed_scores, block_mask, block_row, block_col, block_live):
    slots, width = block_mask.shape[0], prior.shape[1]
    vmem = pl.BlockSpec(memory_space=pltpu.VMEM)
    smem = pl.BlockSpec(memory_space=pltpu.SMEM)
    bf16, f32 = jnp.bfloat16, jnp.float32
    targets, sources = 4 * NY * BLK, 2 * NZ * BLK
    return pl.pallas_call(
        kernel,
        out_shape=jax.ShapeDtypeStruct(prior.shape, bf16),
        in_specs=[vmem, vmem, vmem, vmem, pl.BlockSpec(memory_space=pl.ANY), smem, smem, smem],
        out_specs=vmem,
        scratch_shapes=[
            pltpu.VMEM((slots, BLK, BLK), jnp.int32),
            pltpu.VMEM((slots + 1, BLK, BLK), bf16),
            pltpu.VMEM((targets, sources), bf16),
            pltpu.VMEM((ITERS, sources, width), bf16),
            pltpu.VMEM((ITERS, targets // 2, width), bf16),
            pltpu.VMEM((ITERS, targets // 2, width), bf16),
            pltpu.VMEM((targets, width), f32),
            pltpu.VMEM((ITERS, 2, 8, BLK, width), bf16),
            pltpu.VMEM((ITERS, 2, 8, BLK, width), bf16),
            pltpu.VMEM((ITERS, BLK, width), bf16),
            pltpu.VMEM((ITERS, BLK, width), bf16),
            pltpu.VMEM((BLK, width), f32),
            pltpu.VMEM((BLK, width), f32),
            pltpu.VMEM((BLK, width), f32),
            pltpu.VMEM((BLK, width), f32),
            pltpu.VMEM((8, 128), jnp.int32),
            pltpu.SMEM((8, 128), jnp.int32),
            pltpu.SemaphoreType.DMA((COPIES,)),
            pltpu.SemaphoreType.DMA((COPIES,)),
            pltpu.SemaphoreType.DMA((2,)),
        ],
        compiler_params=pltpu.CompilerParams(
            collective_id=0, has_side_effects=True, vmem_limit_bytes=56 * 1024 * 1024
        ),
        name="propagate",
    )(
        prior,
        inv_degree.reshape(1, -1),
        seed_rows.reshape(1, -1),
        seed_scores,
        block_mask,
        block_row,
        block_col,
        block_live,
    )


def solution(mesh):
    return jax.shard_map(
        local,
        mesh=mesh,
        in_specs=(
            P(("row", "col"), None),
            P(("row", "col")),
            P(("row", "col")),
            P(("row", "col"), None),
            P(("row", "col"), None, None),
            P(("row", "col")),
            P(("row", "col")),
            P(("row", "col")),
        ),
        out_specs=P(("row", "col"), None),
        check_vma=False,
    )
```

```python
import jax
import jax.numpy as jnp
from jax import lax
from jax.experimental import pallas as pl
from jax.experimental.pallas import tpu as pltpu
from jax.sharding import PartitionSpec as P

ITERS = 2
MIX_RATE = 0.9
BLK = 128
NZ, NY = 8, 8

GROUPS = (
    ((0, 0), (0, 2), (0, 6), (1, 0), (0, 1), (0, 7)),
    ((0, 3), (0, 5), (1, 2), (1, 6), (1, 1), (1, 7)),
    ((0, 4), (1, 3), (1, 5), (1, 4)),
)
SLOTS = sum(GROUPS, ())
ORDER = (4, 3, -3, 2, -2, 1, -1, 0)
PIECES = len(ORDER) * BLK
ROWS = 512


def slot(dx, dz):
    return SLOTS.index((dx, dz % NZ)) * BLK


def kernel(
    prior_hbm, inv_hbm, seed_rows_hbm, seed_scores_hbm, mask_hbm, brow_hbm, bcol_hbm, live_hbm,
    out_ref,
    inv_ref, seed_rows_ref, seed_scores_ref, brow_ref, bcol_ref, live_ref, mask_v, wblk, weights, src, csend, crecv, acc, ysend, yrecv,
    base, factor, covered, table_v, table_s, send_sem, recv_sem, local_sem,
):
    f32, bf16 = jnp.float32, jnp.bfloat16
    width = out_ref.shape[1]
    row, col = lax.axis_index("row"), lax.axis_index("col")
    core = row % 2
    y = (row // 2) % NY
    xh = row // (2 * NY)
    z = col % NZ
    xl = col // NZ
    slots = mask_v.shape[0]

    def rowof(a, b, c):
        return (a * NY + b) * 2 + c

    def along_z(d):
        return (row, xl * NZ + (z + d + NZ) % NZ)

    def along_y(d):
        return (rowof(xh, (y + d + NY) % NY, core), col)

    peers = {
        "X": (row, (1 - xl) * NZ + z),
        "C": (rowof(xh, y, 1 - core), col),
        "H": (rowof(1 - xh, y, core), col),
    }
    for d in (1, 2, -1, -2):
        peers["z", d] = along_z(d)
        peers["y", d] = along_y(d)
    for d in (1, -1):
        peers["h", d] = (rowof(1 - xh, (y + d + NY) % NY, core), col)

    barrier = pltpu.get_barrier_semaphore()
    for peer in peers.values():
        pl.semaphore_signal(barrier, inc=1, device_id=peer, device_id_type=pl.DeviceIdType.MESH)

    own_rows = pl.ds(slot(0, 0), BLK)
    fetches = [
        pltpu.make_async_copy(source, target, local_sem.at[2 + n])
        for n, (source, target) in enumerate((
            (brow_hbm, brow_ref),
            (bcol_hbm, bcol_ref),
            (live_hbm, live_ref),
            (prior_hbm, src.at[0, own_rows]),
            (inv_hbm, inv_ref),
            (seed_rows_hbm, seed_rows_ref),
            (seed_scores_hbm, seed_scores_ref),
        ))
    ]
    for fetch in fetches:
        fetch.start()
    mask_copy = pltpu.make_async_copy(mask_hbm, mask_v, local_sem.at[0])
    mask_copy.start()

    started = []

    def send(source, target, peer):
        n = len(started)
        copy = pltpu.make_async_remote_copy(
            src_ref=source,
            dst_ref=target,
            send_sem=send_sem.at[n],
            recv_sem=recv_sem.at[n],
            device_id=peers[peer],
            device_id_type=pl.DeviceIdType.MESH,
        )
        copy.start()
        started.append(copy)
        return copy

    def prepare_table():
        q = lax.broadcasted_iota(jnp.int32, (8, 128), 0)
        lane = lax.broadcasted_iota(jnp.int32, (8, 128), 1)
        p, place = lane // len(SLOTS), lane % len(SLOTS)
        j, dx, dz = (jnp.zeros((8, 128), jnp.int32) for _ in range(3))
        for n, value in enumerate(ORDER):
            j = jnp.where(p == n, value, j)
        for n, pos in enumerate(SLOTS):
            dx = jnp.where(place == n, pos[0], dx)
            dz = jnp.where(place == n, pos[1], dz)
        b = rowof((xh + 1 + q % 2) % 2, (y + j + NY) % NY, (core + 1 + q // 2) % 2)
        spot = jnp.where(q < 4, b * (2 * NZ) + ((xl + dx) % 2) * NZ + (z + dz) % NZ, -2)
        live = live_ref[0]

        def mark(s, table):
            key = brow_ref[s] * (2 * NZ) + bcol_ref[s]
            key = jnp.where(s < live, key, -1)
            return jnp.where(spot == key, s + 1, table)

        table_v[...] = lax.fori_loop(0, slots, mark, jnp.zeros((8, 128), jnp.int32))
        copy = pltpu.make_async_copy(table_v, table_s, local_sem.at[1])
        copy.start()
        return copy

    def prepare_labels():
        docs = lax.broadcasted_iota(jnp.int32, (BLK, seed_rows_ref.shape[1]), 0)
        hits = (docs == seed_rows_ref[...]).astype(f32)
        seeded = jnp.dot(hits.astype(bf16), seed_scores_ref[...], preferred_element_type=f32)
        cov = jnp.broadcast_to(jnp.sum(hits, axis=1, keepdims=True), (BLK, width))
        covered[...] = cov
        eye = lax.broadcasted_iota(jnp.int32, (BLK, BLK), 0) == lax.broadcasted_iota(
            jnp.int32, (BLK, BLK), 1
        )
        inv = jnp.sum(jnp.where(eye, inv_ref[...], 0.0), axis=1, keepdims=True)
        factor[...] = jnp.broadcast_to(MIX_RATE * inv, (BLK, width))
        base[...] = jnp.where(cov > 0.5, seeded, (1.0 - MIX_RATE) * src[0, 0:BLK, :].astype(f32))

    def convert():
        mask_copy.wait()
        wblk[0] = jnp.zeros((BLK, BLK), bf16)

        @pl.loop(0, slots)
        def _(s):
            wblk[s + 1] = mask_v[s].astype(f32).astype(bf16)

    def build(group):
        @pl.loop(0, 4)
        def _(q):
            for p in range(len(ORDER)):
                first = pl.multiple_of(q * PIECES + p * BLK, BLK)
                for pos in group:
                    which = table_s[q, p * len(SLOTS) + SLOTS.index(pos)]
                    weights[pl.ds(first, BLK), slot(*pos) : slot(*pos) + BLK] = wblk[which]

    def product(it, n, first):
        k = slot(*GROUPS[n][0])
        depth = len(GROUPS[n]) * BLK
        return jnp.dot(
            weights[first : first + ROWS, k : k + depth],
            src[it, k : k + depth, :],
            preferred_element_type=f32,
        )

    def products(it, n):
        for first in range(0, 4 * PIECES, ROWS):
            part = product(it, n, first)
            if n:
                part = part + acc[first : first + ROWS, :]
            acc[first : first + ROWS, :] = part

    half = BLK // 2
    pl.semaphore_wait(barrier, len(peers))

    for it in range(ITERS):
        coming = {}

        def block(pos, part):
            return src.at[it, pl.ds(slot(*pos) + part * half, half)]

        def take(dx, dz, part):
            copy = coming.pop((dx, dz % NZ, part), None)
            if copy is not None:
                copy.wait_recv()

        def pass_on(dx, dz, part, way, there):
            take(dx, dz, part)
            source = block((dx, dz), part)
            if it == 0 and (dx, dz) == (0, 0):
                source = prior_hbm.at[pl.ds(part * half, half)]
            coming[there[0], there[1] % NZ, part] = send(source, block(there, part), way)

        for part in (0, 1):
            pass_on(0, 0, part, ("z", 2), (0, -2))
            pass_on(0, 0, part, ("z", -2), (0, 2))
            pass_on(0, 0, part, "X", (1, 0))
        for part in (0, 1):
            pass_on(0, 0, part, ("z", 1), (0, -1))
            pass_on(0, 0, part, ("z", -1), (0, 1))
        if it == 0:
            for fetch in fetches:
                fetch.wait()
            table_copy = prepare_table()
            convert()
            table_copy.wait()
        for part in (0, 1):
            for d in (-2, 2):
                s = -1 if d > 0 else 1
                pass_on(0, d, part, "X", (1, d))
                pass_on(0, d, part, ("z", s), (0, d - s))
                if (part == 0) == (d < 0):
                    pass_on(0, d, part, ("z", 2 * s), (0, 4))
        for part in (0, 1):
            for d in (-1, 1):
                pass_on(0, d, part, "X", (1, d))
        if it == 0:
            build(GROUPS[0])
            build(GROUPS[1])
        else:
            for part in (0, 1):
                take(1, 0, part)
            products(it, 0)
        for part in (0, 1):
            for d in (-2, 2):
                s = -1 if d > 0 else 1
                pass_on(1, d, part, ("z", s), (1, d - s))
                if (part == 0) == (d > 0):
                    pass_on(1, d, part, ("z", 2 * s), (1, 4))
        if it == 0:
            for part in (0, 1):
                take(1, 0, part)
            build(GROUPS[2])
            products(it, 0)
        for dx, dz in GROUPS[1]:
            for part in (0, 1):
                take(dx, dz, part)
        products(it, 1)
        for dx, dz in GROUPS[2]:
            for part in (0, 1):
                take(dx, dz, part)

        core_copies = {}

        def finish(kk, xx):
            for first in range(xx * PIECES, (xx + 1) * PIECES, ROWS):
                at = kk * 2 * PIECES + first
                part = product(it, 2, at) + acc[at : at + ROWS, :]
                if kk:
                    acc[at : at + ROWS, :] = part
                else:
                    csend[it, first : first + ROWS, :] = part.astype(bf16)
                    where = pl.ds(first, ROWS)
                    core_copies[first // ROWS] = send(
                        csend.at[it, where], crecv.at[it, where], "C"
                    )

        def local(j, xx, top=0, rows=BLK):
            first = xx * PIECES + ORDER.index(j) * BLK + top
            copy = core_copies.pop(first // ROWS, None)
            if copy is not None:
                copy.wait_recv()
            at = 2 * PIECES + first
            return acc[at : at + rows, :] + crecv[it, first : first + rows, :].astype(f32)

        sent = {}

        def ship(n, xx, value, way, rows=BLK):
            ysend[it, xx, n, 0:rows, :] = value.astype(bf16)
            where = pl.ds(0, rows)
            sent[n, xx] = send(ysend.at[it, xx, n, where], yrecv.at[it, xx, n, where], way)

        def landed(n, xx, rows=BLK):
            sent.pop((n, xx)).wait_recv()
            return yrecv[it, xx, n, 0:rows, :].astype(f32)

        def far(xx):
            ship(0, xx, local(4, xx, 0, half), ("y", 2), half)
            ship(1, xx, local(4, xx, half, half), ("y", -2), half)
            ship(2, xx, local(3, xx), ("y", 1))
            ship(3, xx, local(-3, xx), ("y", -1))

        def across():
            ship(4, 0, local(1, 0), "H")
            ship(5, 0, local(-1, 0), "H")
            ship(8, 0, local(0, 0), "H")

        def middle(xx):
            total = local(2, xx) + landed(2, xx)
            ship(
                6, xx,
                jnp.concatenate([total[:half] + landed(0, xx, half), total[half:]], axis=0),
                ("yh"[xx == 0], 1),
            )
            total = local(-2, xx) + landed(3, xx)
            ship(
                7, xx,
                jnp.concatenate([total[:half], total[half:] + landed(1, xx, half)], axis=0),
                ("yh"[xx == 0], -1),
            )

        def near(n, d):
            total = local(d, 1) + landed(4 + n, 0) + landed(6 + n, 0) + landed(6 + n, 1)
            ship(4 + n, 1, total, ("y", d))

        finish(0, 0)
        finish(1, 0)
        far(0)
        finish(0, 1)
        finish(1, 1)
        far(1)
        across()
        if it == 0:
            prepare_labels()
        middle(0)
        middle(1)
        near(0, 1)
        near(1, -1)
        total = local(0, 1) + landed(8, 0)
        total = total + landed(4, 1) + landed(5, 1)
        mixed = jnp.where(covered[...] > 0.5, base[...], factor[...] * total + base[...])
        if it == ITERS - 1:
            out_ref[...] = mixed.astype(bf16)
        else:
            src[it + 1, slot(0, 0) : slot(0, 0) + BLK, :] = mixed.astype(bf16)

    for copy in started:
        copy.wait_send()


COPIES = (30 + 4 + 17) * ITERS


def local(prior, inv_degree, seed_rows, seed_scores, block_mask, block_row, block_col, block_live):
    slots, width = block_mask.shape[0], prior.shape[1]
    bf16, f32 = jnp.bfloat16, jnp.float32
    targets, sources = 4 * NY * BLK, 2 * NZ * BLK
    return pl.pallas_call(
        kernel,
        out_shape=jax.ShapeDtypeStruct(prior.shape, bf16),
        in_specs=[pl.BlockSpec(memory_space=pl.ANY)] * 8,
        out_specs=pl.BlockSpec(memory_space=pltpu.VMEM),
        scratch_shapes=[
            pltpu.VMEM((1, inv_degree.shape[0]), f32),
            pltpu.VMEM((1, seed_rows.shape[0]), jnp.int32),
            pltpu.VMEM(seed_scores.shape, bf16),
            pltpu.SMEM(block_row.shape, jnp.int32),
            pltpu.SMEM(block_col.shape, jnp.int32),
            pltpu.SMEM(block_live.shape, jnp.int32),
            pltpu.VMEM((slots, BLK, BLK), jnp.int32),
            pltpu.VMEM((slots + 1, BLK, BLK), bf16),
            pltpu.VMEM((targets, sources), bf16),
            pltpu.VMEM((ITERS, sources, width), bf16),
            pltpu.VMEM((ITERS, targets // 2, width), bf16),
            pltpu.VMEM((ITERS, targets // 2, width), bf16),
            pltpu.VMEM((targets, width), f32),
            pltpu.VMEM((ITERS, 2, 9, BLK, width), bf16),
            pltpu.VMEM((ITERS, 2, 9, BLK, width), bf16),
            pltpu.VMEM((BLK, width), f32),
            pltpu.VMEM((BLK, width), f32),
            pltpu.VMEM((BLK, width), f32),
            pltpu.VMEM((8, 128), jnp.int32),
            pltpu.SMEM((8, 128), jnp.int32),
            pltpu.SemaphoreType.DMA((COPIES,)),
            pltpu.SemaphoreType.DMA((COPIES,)),
            pltpu.SemaphoreType.DMA((9,)),
        ],
        compiler_params=pltpu.CompilerParams(
            collective_id=0, has_side_effects=True, vmem_limit_bytes=56 * 1024 * 1024
        ),
        name="propagate",
    )(
        prior,
        inv_degree.reshape(1, -1),
        seed_rows.reshape(1, -1),
        seed_scores,
        block_mask,
        block_row,
        block_col,
        block_live,
    )


def solution(mesh):
    return jax.shard_map(
        local,
        mesh=mesh,
        in_specs=(
            P(("row", "col"), None),
            P(("row", "col")),
            P(("row", "col")),
            P(("row", "col"), None),
            P(("row", "col"), None, None),
            P(("row", "col")),
            P(("row", "col")),
            P(("row", "col")),
        ),
        out_specs=P(("row", "col"), None),
        check_vma=False,
    )
```

```python
import jax
import jax.numpy as jnp
from jax import lax
from jax.experimental import pallas as pl
from jax.experimental.pallas import tpu as pltpu
from jax.sharding import PartitionSpec as P

ITERS = 2
MIX_RATE = 0.9
BLK = 128
NZ, NY = 8, 8

GROUPS = (
    ((0, 0), (0, 2), (0, 6), (1, 0), (0, 1), (0, 7)),
    ((0, 3), (0, 5), (1, 2), (1, 6), (1, 1), (1, 7)),
    ((0, 4), (1, 3), (1, 5), (1, 4)),
)
SLOTS = sum(GROUPS, ())
ORDER = (4, 3, -3, 2, -2, 1, -1, 0)
PIECES = len(ORDER) * BLK
ROWS = 512


def slot(dx, dz):
    return SLOTS.index((dx, dz % NZ)) * BLK


def kernel(
    prior_hbm, inv_hbm, seed_rows_hbm, seed_scores_hbm, mask_hbm, brow_hbm, bcol_hbm, live_hbm,
    out_ref,
    inv_ref, seed_rows_ref, seed_scores_ref, brow_ref, bcol_ref, live_ref, mask_v, wblk, weights, src, csend, crecv, acc, ysend, yrecv,
    base, factor, covered, table_v, table_s, send_sem, recv_sem, local_sem,
):
    f32, bf16 = jnp.float32, jnp.bfloat16
    width = out_ref.shape[1]
    row, col = lax.axis_index("row"), lax.axis_index("col")
    core = row % 2
    y = (row // 2) % NY
    xh = row // (2 * NY)
    z = col % NZ
    xl = col // NZ
    slots = mask_v.shape[0]

    def rowof(a, b, c):
        return (a * NY + b) * 2 + c

    def along_z(d):
        return (row, xl * NZ + (z + d + NZ) % NZ)

    def along_y(d):
        return (rowof(xh, (y + d + NY) % NY, core), col)

    peers = {
        "X": (row, (1 - xl) * NZ + z),
        "C": (rowof(xh, y, 1 - core), col),
        "H": (rowof(1 - xh, y, core), col),
    }
    for d in (1, 2, -1, -2):
        peers["z", d] = along_z(d)
        peers["y", d] = along_y(d)
    for d in (1, -1):
        peers["h", d] = (rowof(1 - xh, (y + d + NY) % NY, core), col)

    barrier = pltpu.get_barrier_semaphore()
    for peer in peers.values():
        pl.semaphore_signal(barrier, inc=1, device_id=peer, device_id_type=pl.DeviceIdType.MESH)

    own_rows = pl.ds(slot(0, 0), BLK)
    fetches = [
        pltpu.make_async_copy(source, target, local_sem.at[2 + n])
        for n, (source, target) in enumerate((
            (brow_hbm, brow_ref),
            (bcol_hbm, bcol_ref),
            (live_hbm, live_ref),
            (prior_hbm, src.at[0, own_rows]),
            (inv_hbm, inv_ref),
            (seed_rows_hbm, seed_rows_ref),
            (seed_scores_hbm, seed_scores_ref),
        ))
    ]
    for fetch in fetches:
        fetch.start()
    quarter = slots // 4
    mask_copies = []
    for n in range(4):
        where = pl.ds(n * quarter, quarter if n < 3 else slots - 3 * quarter)
        mask_copies.append(
            pltpu.make_async_copy(mask_hbm.at[where], mask_v.at[where], local_sem.at[9 + n])
        )
        mask_copies[n].start()

    started = []

    def send(source, target, peer):
        n = len(started)
        copy = pltpu.make_async_remote_copy(
            src_ref=source,
            dst_ref=target,
            send_sem=send_sem.at[n],
            recv_sem=recv_sem.at[n],
            device_id=peers[peer],
            device_id_type=pl.DeviceIdType.MESH,
        )
        copy.start()
        started.append(copy)
        return copy

    def prepare_table():
        q = lax.broadcasted_iota(jnp.int32, (8, 128), 0)
        lane = lax.broadcasted_iota(jnp.int32, (8, 128), 1)
        p, place = lane // len(SLOTS), lane % len(SLOTS)
        j, dx, dz = (jnp.zeros((8, 128), jnp.int32) for _ in range(3))
        for n, value in enumerate(ORDER):
            j = jnp.where(p == n, value, j)
        for n, pos in enumerate(SLOTS):
            dx = jnp.where(place == n, pos[0], dx)
            dz = jnp.where(place == n, pos[1], dz)
        b = rowof((xh + 1 + q % 2) % 2, (y + j + NY) % NY, (core + 1 + q // 2) % 2)
        spot = jnp.where(q < 4, b * (2 * NZ) + ((xl + dx) % 2) * NZ + (z + dz) % NZ, -2)
        live = live_ref[0]

        def mark(s, table):
            key = brow_ref[s] * (2 * NZ) + bcol_ref[s]
            key = jnp.where(s < live, key, -1)
            return jnp.where(spot == key, s + 1, table)

        table_v[...] = lax.fori_loop(
            0, slots, mark, jnp.zeros((8, 128), jnp.int32), unroll=8
        )
        copy = pltpu.make_async_copy(table_v, table_s, local_sem.at[1])
        copy.start()
        return copy

    def prepare_labels():
        docs = lax.broadcasted_iota(jnp.int32, (BLK, seed_rows_ref.shape[1]), 0)
        hits = (docs == seed_rows_ref[...]).astype(f32)
        seeded = jnp.dot(hits.astype(bf16), seed_scores_ref[...], preferred_element_type=f32)
        cov = jnp.broadcast_to(jnp.sum(hits, axis=1, keepdims=True), (BLK, width))
        covered[...] = cov
        eye = lax.broadcasted_iota(jnp.int32, (BLK, BLK), 0) == lax.broadcasted_iota(
            jnp.int32, (BLK, BLK), 1
        )
        inv = jnp.sum(jnp.where(eye, inv_ref[...], 0.0), axis=1, keepdims=True)
        factor[...] = jnp.broadcast_to(MIX_RATE * inv, (BLK, width))
        base[...] = jnp.where(cov > 0.5, seeded, (1.0 - MIX_RATE) * src[0, 0:BLK, :].astype(f32))

    def convert():
        for copy in mask_copies:
            copy.wait()
        wblk[0] = jnp.zeros((BLK, BLK), bf16)

        @pl.loop(0, slots, unroll=4)
        def _(s):
            wblk[s + 1] = mask_v[s].astype(f32).astype(bf16)

    def build(group):
        @pl.loop(0, 4)
        def _(q):
            for p in range(len(ORDER)):
                first = pl.multiple_of(q * PIECES + p * BLK, BLK)
                for pos in group:
                    which = table_s[q, p * len(SLOTS) + SLOTS.index(pos)]
                    weights[pl.ds(first, BLK), slot(*pos) : slot(*pos) + BLK] = wblk[which]

    def product(it, n, first):
        k = slot(*GROUPS[n][0])
        depth = len(GROUPS[n]) * BLK
        return jnp.dot(
            weights[first : first + ROWS, k : k + depth],
            src[it, k : k + depth, :],
            preferred_element_type=f32,
        )

    def products(it, n):
        for first in range(0, 4 * PIECES, ROWS):
            part = product(it, n, first)
            if n:
                part = part + acc[first : first + ROWS, :]
            acc[first : first + ROWS, :] = part

    half = BLK // 2
    pl.semaphore_wait(barrier, len(peers))

    for it in range(ITERS):
        coming = {}

        def block(pos, part):
            return src.at[it, pl.ds(slot(*pos) + part * half, half)]

        def take(dx, dz, part):
            copy = coming.pop((dx, dz % NZ, part), None)
            if copy is not None:
                copy.wait_recv()

        def pass_on(dx, dz, part, way, there):
            take(dx, dz, part)
            source = block((dx, dz), part)
            if it == 0 and (dx, dz) == (0, 0):
                source = prior_hbm.at[pl.ds(part * half, half)]
            coming[there[0], there[1] % NZ, part] = send(source, block(there, part), way)

        for part in (0, 1):
            pass_on(0, 0, part, ("z", 2), (0, -2))
            pass_on(0, 0, part, ("z", -2), (0, 2))
            pass_on(0, 0, part, "X", (1, 0))
        for part in (0, 1):
            pass_on(0, 0, part, ("z", 1), (0, -1))
            pass_on(0, 0, part, ("z", -1), (0, 1))
        if it == 0:
            for fetch in fetches:
                fetch.wait()
            table_copy = prepare_table()
            convert()
            table_copy.wait()
        for part in (0, 1):
            for d in (-2, 2):
                s = -1 if d > 0 else 1
                pass_on(0, d, part, "X", (1, d))
                pass_on(0, d, part, ("z", s), (0, d - s))
                if (part == 0) == (d < 0):
                    pass_on(0, d, part, ("z", 2 * s), (0, 4))
        for part in (0, 1):
            for d in (-1, 1):
                pass_on(0, d, part, "X", (1, d))
        if it == 0:
            build(GROUPS[0])
            build(GROUPS[1])
        else:
            for part in (0, 1):
                take(1, 0, part)
            products(it, 0)
        for part in (0, 1):
            for d in (-2, 2):
                s = -1 if d > 0 else 1
                pass_on(1, d, part, ("z", s), (1, d - s))
                if (part == 0) == (d > 0):
                    pass_on(1, d, part, ("z", 2 * s), (1, 4))
        if it == 0:
            for part in (0, 1):
                take(1, 0, part)
            build(GROUPS[2])
            products(it, 0)
        for dx, dz in GROUPS[1]:
            for part in (0, 1):
                take(dx, dz, part)
        products(it, 1)
        for dx, dz in GROUPS[2]:
            for part in (0, 1):
                take(dx, dz, part)

        core_copies = {}

        def finish(kk, xx, n):
            first = xx * PIECES + n * ROWS
            at = kk * 2 * PIECES + first
            part = product(it, 2, at) + acc[at : at + ROWS, :]
            if kk:
                acc[at : at + ROWS, :] = part
            else:
                csend[it, first : first + ROWS, :] = part.astype(bf16)
                where = pl.ds(first, ROWS)
                core_copies[first // ROWS] = send(csend.at[it, where], crecv.at[it, where], "C")

        def local(j, xx, top=0, rows=BLK):
            first = xx * PIECES + ORDER.index(j) * BLK + top
            copy = core_copies.pop(first // ROWS, None)
            if copy is not None:
                copy.wait_recv()
            at = 2 * PIECES + first
            return acc[at : at + rows, :] + crecv[it, first : first + rows, :].astype(f32)

        sent = {}

        def ship(n, xx, value, way, rows=BLK):
            ysend[it, xx, n, 0:rows, :] = value.astype(bf16)
            where = pl.ds(0, rows)
            sent[n, xx] = send(ysend.at[it, xx, n, where], yrecv.at[it, xx, n, where], way)

        def landed(n, xx, rows=BLK):
            sent.pop((n, xx)).wait_recv()
            return yrecv[it, xx, n, 0:rows, :].astype(f32)

        def far(xx):
            ship(0, xx, local(4, xx, 0, half), ("y", 2), half)
            ship(1, xx, local(4, xx, half, half), ("y", -2), half)
            ship(2, xx, local(3, xx), ("y", 1))
            ship(3, xx, local(-3, xx), ("y", -1))

        def across():
            ship(4, 0, local(1, 0), "H")
            ship(5, 0, local(-1, 0), "H")
            ship(8, 0, local(0, 0), "H")

        def middle(xx):
            total = local(2, xx) + landed(2, xx)
            ship(
                6, xx,
                jnp.concatenate([total[:half] + landed(0, xx, half), total[half:]], axis=0),
                ("yh"[xx == 0], 1),
            )
            total = local(-2, xx) + landed(3, xx)
            ship(
                7, xx,
                jnp.concatenate([total[:half], total[half:] + landed(1, xx, half)], axis=0),
                ("yh"[xx == 0], -1),
            )

        def near(n, d):
            total = local(d, 1) + landed(4 + n, 0) + landed(6 + n, 0) + landed(6 + n, 1)
            ship(4 + n, 1, total, ("y", d))

        for kk in (0, 1):
            for xx in (0, 1):
                finish(kk, xx, 0)
        far(0)
        far(1)
        for kk in (0, 1):
            for xx in (0, 1):
                finish(kk, xx, 1)
        across()
        if it == 0:
            prepare_labels()
        middle(0)
        middle(1)
        near(0, 1)
        near(1, -1)
        total = local(0, 1) + landed(8, 0)
        total = total + landed(4, 1) + landed(5, 1)
        mixed = jnp.where(covered[...] > 0.5, base[...], factor[...] * total + base[...])
        if it == ITERS - 1:
            out_ref[...] = mixed.astype(bf16)
        else:
            src[it + 1, slot(0, 0) : slot(0, 0) + BLK, :] = mixed.astype(bf16)

    for copy in started:
        copy.wait_send()


COPIES = (30 + 4 + 17) * ITERS


def local(prior, inv_degree, seed_rows, seed_scores, block_mask, block_row, block_col, block_live):
    slots, width = block_mask.shape[0], prior.shape[1]
    bf16, f32 = jnp.bfloat16, jnp.float32
    targets, sources = 4 * NY * BLK, 2 * NZ * BLK
    return pl.pallas_call(
        kernel,
        out_shape=jax.ShapeDtypeStruct(prior.shape, bf16),
        in_specs=[pl.BlockSpec(memory_space=pl.ANY)] * 8,
        out_specs=pl.BlockSpec(memory_space=pltpu.VMEM),
        scratch_shapes=[
            pltpu.VMEM((1, inv_degree.shape[0]), f32),
            pltpu.VMEM((1, seed_rows.shape[0]), jnp.int32),
            pltpu.VMEM(seed_scores.shape, bf16),
            pltpu.SMEM(block_row.shape, jnp.int32),
            pltpu.SMEM(block_col.shape, jnp.int32),
            pltpu.SMEM(block_live.shape, jnp.int32),
            pltpu.VMEM((slots, BLK, BLK), jnp.int32),
            pltpu.VMEM((slots + 1, BLK, BLK), bf16),
            pltpu.VMEM((targets, sources), bf16),
            pltpu.VMEM((ITERS, sources, width), bf16),
            pltpu.VMEM((ITERS, targets // 2, width), bf16),
            pltpu.VMEM((ITERS, targets // 2, width), bf16),
            pltpu.VMEM((targets, width), f32),
            pltpu.VMEM((ITERS, 2, 9, BLK, width), bf16),
            pltpu.VMEM((ITERS, 2, 9, BLK, width), bf16),
            pltpu.VMEM((BLK, width), f32),
            pltpu.VMEM((BLK, width), f32),
            pltpu.VMEM((BLK, width), f32),
            pltpu.VMEM((8, 128), jnp.int32),
            pltpu.SMEM((8, 128), jnp.int32),
            pltpu.SemaphoreType.DMA((COPIES,)),
            pltpu.SemaphoreType.DMA((COPIES,)),
            pltpu.SemaphoreType.DMA((13,)),
        ],
        compiler_params=pltpu.CompilerParams(
            collective_id=0, has_side_effects=True, vmem_limit_bytes=56 * 1024 * 1024
        ),
        name="propagate",
    )(
        prior,
        inv_degree.reshape(1, -1),
        seed_rows.reshape(1, -1),
        seed_scores,
        block_mask,
        block_row,
        block_col,
        block_live,
    )


def solution(mesh):
    return jax.shard_map(
        local,
        mesh=mesh,
        in_specs=(
            P(("row", "col"), None),
            P(("row", "col")),
            P(("row", "col")),
            P(("row", "col"), None),
            P(("row", "col"), None, None),
            P(("row", "col")),
            P(("row", "col")),
            P(("row", "col")),
        ),
        out_specs=P(("row", "col"), None),
        check_vma=False,
    )
```

```python
import jax
import jax.numpy as jnp
from jax import lax
from jax.experimental import pallas as pl
from jax.experimental.pallas import tpu as pltpu
from jax.sharding import PartitionSpec as P

ITERS = 2
MIX_RATE = 0.9
BLK = 128
NZ, NY = 8, 8

GROUPS = (
    ((0, 0), (0, 2), (0, 6), (1, 0), (0, 1), (0, 7)),
    ((0, 3), (0, 5), (1, 2), (1, 6), (1, 1), (1, 7)),
    ((0, 4), (1, 3), (1, 5), (1, 4)),
)
SLOTS = sum(GROUPS, ())
ORDER = (4, 3, -3, 2, -2, 1, -1, 0)
PIECES = len(ORDER) * BLK
ROWS = 512


def slot(dx, dz):
    return SLOTS.index((dx, dz % NZ)) * BLK


def kernel(
    prior_hbm, inv_hbm, seed_rows_hbm, seed_scores_hbm, mask_hbm, brow_hbm, bcol_hbm, live_hbm,
    out_ref,
    inv_ref, seed_rows_ref, seed_scores_ref, brow_ref, bcol_ref, live_ref, mask_v, wblk, weights, src, csend, crecv, acc, ysend, yrecv,
    base, factor, covered, table_v, table_s, send_sem, recv_sem, local_sem,
):
    f32, bf16 = jnp.float32, jnp.bfloat16
    width = out_ref.shape[1]
    row, col = lax.axis_index("row"), lax.axis_index("col")
    core = row % 2
    y = (row // 2) % NY
    xh = row // (2 * NY)
    z = col % NZ
    xl = col // NZ
    slots = mask_v.shape[0]

    def rowof(a, b, c):
        return (a * NY + b) * 2 + c

    def along_z(d):
        return (row, xl * NZ + (z + d + NZ) % NZ)

    def along_y(d):
        return (rowof(xh, (y + d + NY) % NY, core), col)

    peers = {
        "X": (row, (1 - xl) * NZ + z),
        "C": (rowof(xh, y, 1 - core), col),
        "H": (rowof(1 - xh, y, core), col),
    }
    for d in (1, 2, -1, -2):
        peers["z", d] = along_z(d)
        peers["y", d] = along_y(d)
    for d in (1, -1):
        peers["h", d] = (rowof(1 - xh, (y + d + NY) % NY, core), col)

    barrier = pltpu.get_barrier_semaphore()
    for peer in peers.values():
        pl.semaphore_signal(barrier, inc=1, device_id=peer, device_id_type=pl.DeviceIdType.MESH)

    own_rows = pl.ds(slot(0, 0), BLK)
    fetches = [
        pltpu.make_async_copy(source, target, local_sem.at[2 + n])
        for n, (source, target) in enumerate((
            (brow_hbm, brow_ref),
            (bcol_hbm, bcol_ref),
            (live_hbm, live_ref),
            (prior_hbm, src.at[0, own_rows]),
            (inv_hbm, inv_ref),
            (seed_rows_hbm, seed_rows_ref),
            (seed_scores_hbm, seed_scores_ref),
        ))
    ]
    for fetch in fetches:
        fetch.start()
    quarter = slots // 4
    mask_copies = []
    for n in range(4):
        where = pl.ds(n * quarter, quarter if n < 3 else slots - 3 * quarter)
        mask_copies.append(
            pltpu.make_async_copy(mask_hbm.at[where], mask_v.at[where], local_sem.at[9 + n])
        )
        mask_copies[n].start()

    started = []

    def send(source, target, peer):
        n = len(started)
        copy = pltpu.make_async_remote_copy(
            src_ref=source,
            dst_ref=target,
            send_sem=send_sem.at[n],
            recv_sem=recv_sem.at[n],
            device_id=peers[peer],
            device_id_type=pl.DeviceIdType.MESH,
        )
        copy.start()
        started.append(copy)
        return copy

    def prepare_table():
        q = lax.broadcasted_iota(jnp.int32, (8, 128), 0)
        lane = lax.broadcasted_iota(jnp.int32, (8, 128), 1)
        p, place = lane // len(SLOTS), lane % len(SLOTS)
        j, dx, dz = (jnp.zeros((8, 128), jnp.int32) for _ in range(3))
        for n, value in enumerate(ORDER):
            j = jnp.where(p == n, value, j)
        for n, pos in enumerate(SLOTS):
            dx = jnp.where(place == n, pos[0], dx)
            dz = jnp.where(place == n, pos[1], dz)
        b = rowof((xh + 1 + q % 2) % 2, (y + j + NY) % NY, (core + 1 + q // 2) % 2)
        spot = jnp.where(q < 4, b * (2 * NZ) + ((xl + dx) % 2) * NZ + (z + dz) % NZ, -2)
        live = live_ref[0]

        def mark(s, table):
            key = brow_ref[s] * (2 * NZ) + bcol_ref[s]
            key = jnp.where(s < live, key, -1)
            return jnp.where(spot == key, s + 1, table)

        table_v[...] = lax.fori_loop(
            0, slots, mark, jnp.zeros((8, 128), jnp.int32), unroll=8
        )
        copy = pltpu.make_async_copy(table_v, table_s, local_sem.at[1])
        copy.start()
        return copy

    def prepare_labels():
        docs = lax.broadcasted_iota(jnp.int32, (BLK, seed_rows_ref.shape[1]), 0)
        hits = (docs == seed_rows_ref[...]).astype(f32)
        seeded = jnp.dot(hits.astype(bf16), seed_scores_ref[...], preferred_element_type=f32)
        cov = jnp.broadcast_to(jnp.sum(hits, axis=1, keepdims=True), (BLK, width))
        covered[...] = cov
        eye = lax.broadcasted_iota(jnp.int32, (BLK, BLK), 0) == lax.broadcasted_iota(
            jnp.int32, (BLK, BLK), 1
        )
        inv = jnp.sum(jnp.where(eye, inv_ref[...], 0.0), axis=1, keepdims=True)
        factor[...] = jnp.broadcast_to(MIX_RATE * inv, (BLK, width))
        base[...] = jnp.where(cov > 0.5, seeded, (1.0 - MIX_RATE) * src[0, 0:BLK, :].astype(f32))

    def convert():
        for copy in mask_copies:
            copy.wait()
        wblk[0] = jnp.zeros((BLK, BLK), bf16)

        @pl.loop(0, slots, unroll=4)
        def _(s):
            wblk[s + 1] = mask_v[s].astype(f32).astype(bf16)

    def build(group):
        @pl.loop(0, 4)
        def _(q):
            for p in range(len(ORDER)):
                first = pl.multiple_of(q * PIECES + p * BLK, BLK)
                for pos in group:
                    which = table_s[q, p * len(SLOTS) + SLOTS.index(pos)]
                    weights[pl.ds(first, BLK), slot(*pos) : slot(*pos) + BLK] = wblk[which]

    def product(it, n, first):
        k = slot(*GROUPS[n][0])
        depth = len(GROUPS[n]) * BLK
        return jnp.dot(
            weights[first : first + ROWS, k : k + depth],
            src[it, k : k + depth, :],
            preferred_element_type=f32,
        )

    def products(it, n):
        for first in range(0, 4 * PIECES, ROWS):
            part = product(it, n, first)
            if n:
                part = part + acc[first : first + ROWS, :]
            acc[first : first + ROWS, :] = part

    half = BLK // 2
    pl.semaphore_wait(barrier, len(peers))

    for it in range(ITERS):
        coming = {}

        def block(pos, part):
            return src.at[it, pl.ds(slot(*pos) + part * half, half)]

        def take(dx, dz, part):
            copy = coming.pop((dx, dz % NZ, part), None)
            if copy is not None:
                copy.wait_recv()

        def pass_on(dx, dz, part, way, there):
            take(dx, dz, part)
            source = block((dx, dz), part)
            if it == 0 and (dx, dz) == (0, 0):
                source = prior_hbm.at[pl.ds(part * half, half)]
            coming[there[0], there[1] % NZ, part] = send(source, block(there, part), way)

        for part in (0, 1):
            pass_on(0, 0, part, ("z", 2), (0, -2))
            pass_on(0, 0, part, ("z", -2), (0, 2))
            pass_on(0, 0, part, "X", (1, 0))
        for part in (0, 1):
            pass_on(0, 0, part, ("z", 1), (0, -1))
            pass_on(0, 0, part, ("z", -1), (0, 1))
        if it == 0:
            for fetch in fetches:
                fetch.wait()
            table_copy = prepare_table()
            convert()
            table_copy.wait()
        for part in (0, 1):
            for d in (-2, 2):
                s = -1 if d > 0 else 1
                pass_on(0, d, part, "X", (1, d))
                pass_on(0, d, part, ("z", s), (0, d - s))
                if (part == 0) == (d < 0):
                    pass_on(0, d, part, ("z", 2 * s), (0, 4))
        for part in (0, 1):
            for d in (-1, 1):
                pass_on(0, d, part, "X", (1, d))
        if it == 0:
            build(GROUPS[0])
            build(GROUPS[1])
            build(GROUPS[2])
        else:
            for part in (0, 1):
                take(1, 0, part)
            products(it, 0)
        for part in (0, 1):
            for d in (-2, 2):
                s = -1 if d > 0 else 1
                pass_on(1, d, part, ("z", s), (1, d - s))
                if (part == 0) == (d > 0):
                    pass_on(1, d, part, ("z", 2 * s), (1, 4))
        if it == 0:
            for part in (0, 1):
                take(1, 0, part)
            products(it, 0)
        for dx, dz in GROUPS[1]:
            for part in (0, 1):
                take(dx, dz, part)
        products(it, 1)
        for dx, dz in GROUPS[2]:
            for part in (0, 1):
                take(dx, dz, part)

        core_copies = {}

        def finish(kk, xx, n):
            first = xx * PIECES + n * ROWS
            at = kk * 2 * PIECES + first
            part = product(it, 2, at) + acc[at : at + ROWS, :]
            if kk:
                acc[at : at + ROWS, :] = part
            else:
                csend[it, first : first + ROWS, :] = part.astype(bf16)
                where = pl.ds(first, ROWS)
                core_copies[first // ROWS] = send(csend.at[it, where], crecv.at[it, where], "C")

        def local(j, xx, top=0, rows=BLK):
            first = xx * PIECES + ORDER.index(j) * BLK + top
            copy = core_copies.pop(first // ROWS, None)
            if copy is not None:
                copy.wait_recv()
            at = 2 * PIECES + first
            return acc[at : at + rows, :] + crecv[it, first : first + rows, :].astype(f32)

        sent = {}

        def ship(n, xx, value, way, rows=BLK):
            ysend[it, xx, n, 0:rows, :] = value.astype(bf16)
            where = pl.ds(0, rows)
            sent[n, xx] = send(ysend.at[it, xx, n, where], yrecv.at[it, xx, n, where], way)

        def landed(n, xx, rows=BLK):
            sent.pop((n, xx)).wait_recv()
            return yrecv[it, xx, n, 0:rows, :].astype(f32)

        def far(xx):
            ship(0, xx, local(4, xx, 0, half), ("y", 2), half)
            ship(1, xx, local(4, xx, half, half), ("y", -2), half)
            ship(2, xx, local(3, xx), ("y", 1))
            ship(3, xx, local(-3, xx), ("y", -1))

        def across():
            ship(4, 0, local(1, 0), "H")
            ship(5, 0, local(-1, 0), "H")
            ship(8, 0, local(0, 0), "H")

        def middle(xx):
            total = local(2, xx) + landed(2, xx)
            ship(
                6, xx,
                jnp.concatenate([total[:half] + landed(0, xx, half), total[half:]], axis=0),
                ("yh"[xx == 0], 1),
            )
            total = local(-2, xx) + landed(3, xx)
            ship(
                7, xx,
                jnp.concatenate([total[:half], total[half:] + landed(1, xx, half)], axis=0),
                ("yh"[xx == 0], -1),
            )

        def near(n, d):
            total = local(d, 1) + landed(4 + n, 0) + landed(6 + n, 0) + landed(6 + n, 1)
            ship(4 + n, 1, total, ("y", d))

        for kk in (0, 1):
            for xx in (0, 1):
                finish(kk, xx, 0)
        far(0)
        far(1)
        for kk in (0, 1):
            for xx in (0, 1):
                finish(kk, xx, 1)
        across()
        if it == 0:
            prepare_labels()
        middle(0)
        middle(1)
        near(0, 1)
        near(1, -1)
        total = local(0, 1) + landed(8, 0)
        total = total + landed(4, 1) + landed(5, 1)
        mixed = jnp.where(covered[...] > 0.5, base[...], factor[...] * total + base[...])
        if it == ITERS - 1:
            out_ref[...] = mixed.astype(bf16)
        else:
            src[it + 1, slot(0, 0) : slot(0, 0) + BLK, :] = mixed.astype(bf16)

    for copy in started:
        copy.wait_send()


COPIES = (30 + 4 + 17) * ITERS


def local(prior, inv_degree, seed_rows, seed_scores, block_mask, block_row, block_col, block_live):
    slots, width = block_mask.shape[0], prior.shape[1]
    bf16, f32 = jnp.bfloat16, jnp.float32
    targets, sources = 4 * NY * BLK, 2 * NZ * BLK
    return pl.pallas_call(
        kernel,
        out_shape=jax.ShapeDtypeStruct(prior.shape, bf16),
        in_specs=[pl.BlockSpec(memory_space=pl.ANY)] * 8,
        out_specs=pl.BlockSpec(memory_space=pltpu.VMEM),
        scratch_shapes=[
            pltpu.VMEM((1, inv_degree.shape[0]), f32),
            pltpu.VMEM((1, seed_rows.shape[0]), jnp.int32),
            pltpu.VMEM(seed_scores.shape, bf16),
            pltpu.SMEM(block_row.shape, jnp.int32),
            pltpu.SMEM(block_col.shape, jnp.int32),
            pltpu.SMEM(block_live.shape, jnp.int32),
            pltpu.VMEM((slots, BLK, BLK), jnp.int32),
            pltpu.VMEM((slots + 1, BLK, BLK), bf16),
            pltpu.VMEM((targets, sources), bf16),
            pltpu.VMEM((ITERS, sources, width), bf16),
            pltpu.VMEM((ITERS, targets // 2, width), bf16),
            pltpu.VMEM((ITERS, targets // 2, width), bf16),
            pltpu.VMEM((targets, width), f32),
            pltpu.VMEM((ITERS, 2, 9, BLK, width), bf16),
            pltpu.VMEM((ITERS, 2, 9, BLK, width), bf16),
            pltpu.VMEM((BLK, width), f32),
            pltpu.VMEM((BLK, width), f32),
            pltpu.VMEM((BLK, width), f32),
            pltpu.VMEM((8, 128), jnp.int32),
            pltpu.SMEM((8, 128), jnp.int32),
            pltpu.SemaphoreType.DMA((COPIES,)),
            pltpu.SemaphoreType.DMA((COPIES,)),
            pltpu.SemaphoreType.DMA((13,)),
        ],
        compiler_params=pltpu.CompilerParams(
            collective_id=0, has_side_effects=True, vmem_limit_bytes=56 * 1024 * 1024
        ),
        name="propagate",
    )(
        prior,
        inv_degree.reshape(1, -1),
        seed_rows.reshape(1, -1),
        seed_scores,
        block_mask,
        block_row,
        block_col,
        block_live,
    )


def solution(mesh):
    return jax.shard_map(
        local,
        mesh=mesh,
        in_specs=(
            P(("row", "col"), None),
            P(("row", "col")),
            P(("row", "col")),
            P(("row", "col"), None),
            P(("row", "col"), None, None),
            P(("row", "col")),
            P(("row", "col")),
            P(("row", "col")),
        ),
        out_specs=P(("row", "col"), None),
        check_vma=False,
    )
```
